32 devices in a mesh: groups: 1, slab: 32 (over z, y, x, core).
Axes of the slice: x: 2, y: 2, z: 4, core: 2. Of those that a mesh axis runs over, the one named last changes fastest.
Arguments:
- eigvecs: bfloat16 [32, 2, 3, 128, 512], P(('groups', 'slab')), may hold values from -6 to 6
- links: bfloat16 [32, 3, 2, 3, 3, 512], P(('groups', 'slab')), may hold values from -4 to 4
- momenta: int32 [4, 3], replicated, may hold values from -2 to 2
- directions: int32 [4], replicated, may hold values from 0 to 5, as said below
- pairs: int32 [32, 2], P(('groups', 'slab')), may hold values from 0 to 1
- perambulators: bfloat16 [32, 2, 512, 512], P(('groups', 'slab')), may hold values from -0.25 to 0.25
Outputs:
- elementals: float32 [2048, 128], P(('groups', 'slab'))
- correlators: float32 [32, 4, 2], P(('groups', 'slab'))
The draws below stay inside these ranges and needn't reach their ends.
Inputs may be any that keep to these rules, and one draw needn't show every extreme that they name: `directions`: code 2 a + d is one link step along axis a (0 x, 1 y, 2 z), forward if d = 0 and backward if d = 1; codes 4 and 5 both occur.
All inputs are finite; a program needn't handle non-finite values.
Results may differ from the reference program's by a relative error of at most 0.0057.
Values may be sent and summed in bfloat16 or wider, within the bound.
A program may use at most 128 MiB of HBM per device.

```python
import math
import jax
import jax.numpy as jnp
from jax import lax

NV = 128
SPIN = 4
MOM = 4
LX = 16
LY = 16
LZ = 32
ZBLK = 16
NT = 2
SITES_DEV = 512
SITES = 8192
PAIRS = 32
NS = 512
ROWS = 2048


def draw_directions(key, part):
    first_key, second_key = jax.random.split(jax.random.fold_in(key, 17))
    others = jax.random.randint(first_key, (MOM - 2,), 0, 6).astype(jnp.int32)
    codes = jnp.concatenate([jnp.array([4, 5], dtype=jnp.int32), others])
    order = jax.random.permutation(second_key, MOM)
    return codes[order]


def set_ends(values, own_key, least, high):
    place = [jax.random.randint(jax.random.fold_in(own_key, axis), (), 0, length) for axis, length in enumerate(values.shape)]
    longest = values.shape.index(max(values.shape))
    next_to = place[:longest] + [(place[longest] + 1) % values.shape[longest]] + place[longest + 1:]
    return values.at[tuple(place)].set(least).at[tuple(next_to)].set(high)


def levels(rng, extent, pieces, smallest, top_value):
    def one(dim, parts):
        heights = jax.random.uniform(jax.random.fold_in(jax.random.fold_in(rng, 6), dim), (parts,), jnp.float32, smallest / len(pieces), top_value / len(pieces))
        return jnp.repeat(jnp.exp(heights), extent[dim] // parts).reshape((-1,) + (1,) * (len(extent) - dim - 1))

    loudness = one(*pieces[0])
    for cut in pieces[1:]:
        loudness = loudness * one(*cut)
    return loudness


def gaussian(own_key, shape, spread, limit, cuts=(), held_as=jnp.bfloat16):
    loudness = levels(own_key, shape, cuts, -0.22, 0.18) if cuts else 1.0
    values = jax.random.normal(own_key, shape, jnp.float32) * spread * loudness
    return jnp.minimum(jnp.maximum(values, -limit), limit).astype(held_as)


def setup_inputs(seed: int = 0, part: int = 0) -> dict:
    key_list = jax.random.split(jax.random.key(seed), 7)
    part_keys = jax.random.split(jax.random.fold_in(key_list[6], part), 7)
    return {
        "eigvecs": gaussian(part_keys[0], (ZBLK * NT, 2, 3, NV, SITES_DEV), 1.0, 6.0, ((0, 32),)),
        "links": gaussian(part_keys[1], (ZBLK * NT, 3, 2, 3, 3, SITES_DEV), 0.577, 4.0, ((0, 32),)),
        "momenta": set_ends(jax.random.randint(key_list[2], (MOM, 3), -2, 3), jax.random.fold_in(key_list[2], 1), -2, 2).astype(jnp.int32),
        "directions": draw_directions(jax.random.fold_in(key_list[6], 71), part),
        "pairs": set_ends(jax.random.randint(part_keys[4], (PAIRS, 2), 0, NT), jax.random.fold_in(part_keys[4], 1), 0, NT - 1).astype(jnp.int32),
        "perambulators": gaussian(part_keys[5], (PAIRS, 2, NS, NS), NS ** -0.5, 0.25, ((0, 32),)),
    }


def color_apply(link_field, vectors, adjoint):
    real_rows = []
    imag_rows = []
    for a in range(3):
        terms_real = []
        terms_imag = []
        for b in range(3):
            if adjoint:
                link_real = link_field[..., 0, b, a, :].astype(jnp.float32)
                link_imag = -link_field[..., 1, b, a, :].astype(jnp.float32)
            else:
                link_real = link_field[..., 0, a, b, :].astype(jnp.float32)
                link_imag = link_field[..., 1, a, b, :].astype(jnp.float32)
            link_real = link_real[..., None, :]
            link_imag = link_imag[..., None, :]
            vec_real = vectors[..., 0, b, :, :].astype(jnp.float32)
            vec_imag = vectors[..., 1, b, :, :].astype(jnp.float32)
            terms_real.append(link_real * vec_real - link_imag * vec_imag)
            terms_imag.append(link_real * vec_imag + link_imag * vec_real)
        real_rows.append(terms_real[0] + terms_real[1] + terms_real[2])
        imag_rows.append(terms_imag[0] + terms_imag[1] + terms_imag[2])
    return jnp.stack([jnp.stack(real_rows, axis=-3), jnp.stack(imag_rows, axis=-3)], axis=-4)

def shift_sites(field, axis, step, depth_planes):
    shaped = field.reshape(field.shape[:-1] + (depth_planes, LY, LX))
    moved = jnp.roll(shaped, step, axis=field.ndim + 1 - axis)
    return moved.reshape(field.shape)

def phase_tables(momenta, sites_global, lattice_z):
    xpos = sites_global % LX
    ypos = sites_global // LX % LY
    zpos = sites_global // (LX * LY)
    frac = jnp.mod(momenta[:, 0:1] * xpos[None, :], LX).astype(jnp.float32) / LX
    frac = frac + jnp.mod(momenta[:, 1:2] * ypos[None, :], LY).astype(jnp.float32) / LY
    frac = frac + jnp.mod(momenta[:, 2:3] * zpos[None, :], lattice_z).astype(jnp.float32) / lattice_z
    angle = 2.0 * math.pi * frac
    return (jnp.cos(angle), jnp.sin(angle))

def contract(vectors, displaced, cosine, sine):
    wave_real = displaced[..., 0, :, :, :] * cosine + displaced[..., 1, :, :, :] * sine
    wave_imag = displaced[..., 1, :, :, :] * cosine - displaced[..., 0, :, :, :] * sine
    wave_real = wave_real.astype(jnp.bfloat16).astype(jnp.float32)
    wave_imag = wave_imag.astype(jnp.bfloat16).astype(jnp.float32)
    left_side = vectors.reshape(vectors.shape[:-4] + (6,) + vectors.shape[-2:]).astype(jnp.float32)
    right_real = jnp.concatenate([wave_real, wave_imag], axis=-3)
    right_imag = jnp.concatenate([wave_imag, -wave_real], axis=-3)
    real = jnp.einsum('kis,kjs->ij', left_side, right_real, preferred_element_type=jnp.float32)
    imag = jnp.einsum('kis,kjs->ij', left_side, right_imag, preferred_element_type=jnp.float32)
    return jnp.stack([real, imag], axis=0)

def product(form, left_side, right_side):
    return jnp.einsum(form, left_side.astype(jnp.float32), right_side.astype(jnp.float32), preferred_element_type=jnp.float32)

def correlate(sink, source, peramb, spin_sign):
    tau_rows = peramb.reshape(2, SPIN, NV, NS)
    tau_cols = peramb.reshape(2, NS, SPIN, NV)
    sink_real = product('mij,sjb->msib', sink[:, 0], tau_rows[0]) - product('mij,sjb->msib', sink[:, 1], tau_rows[1])
    sink_imag = product('mij,sjb->msib', sink[:, 0], tau_rows[1]) + product('mij,sjb->msib', sink[:, 1], tau_rows[0])
    cross_real = product('mji,asj->masi', source[:, 0], tau_cols[0]) - product('mji,asj->masi', source[:, 1], tau_cols[1])
    cross_imag = product('mji,asj->masi', source[:, 0], tau_cols[1]) + product('mji,asj->masi', source[:, 1], tau_cols[0])
    sink_real = sink_real.reshape(MOM, NS, NS)
    sink_imag = sink_imag.reshape(MOM, NS, NS)
    cross_real = cross_real.reshape(MOM, NS, NS)
    cross_imag = cross_imag.reshape(MOM, NS, NS)
    weight = spin_sign[:, None] * spin_sign[None, :]
    real = lax.optimization_barrier(jnp.sum(weight * (sink_real * cross_real + sink_imag * cross_imag), axis=(1, 2))) / NS
    imag = lax.optimization_barrier(jnp.sum(weight * (sink_imag * cross_real - sink_real * cross_imag), axis=(1, 2))) / NS
    return jnp.stack([real, imag], axis=-1)

def unblock(array):
    shaped = array.reshape((ZBLK, NT) + array.shape[1:])
    moved = jnp.moveaxis(shaped, 0, -2)
    return moved.reshape((NT,) + array.shape[1:-1] + (SITES,))

def reference(eigvecs, links, momenta, directions, pairs, perambulators):
    full_vecs = unblock(eigvecs)
    full_links = unblock(links)
    sites_global = jnp.arange(SITES, dtype=jnp.int32)
    cosine, sine = phase_tables(momenta, sites_global, LZ)
    scale = 1.0 / math.sqrt(3.0 * SITES)

    def per_time(operands):
        vectors, link_field = operands

        def branch(code):
            axis = code // 2

            def run():
                if code % 2 == 0:
                    return color_apply(link_field[axis], shift_sites(vectors, axis, -1, LZ), False)
                return color_apply(shift_sites(link_field[axis], axis, 1, LZ), shift_sites(vectors, axis, 1, LZ), True)
            return run
        branches = [branch(code) for code in range(6)]
        blocks = []
        for m in range(MOM):
            displaced = lax.switch(directions[m], branches)
            blocks.append(contract(vectors, displaced, cosine[m], sine[m]))
        return jnp.stack(blocks, axis=0) * scale
    elementals = lax.map(per_time, (full_vecs, full_links)).reshape(ROWS, NV)
    phi = elementals.astype(jnp.bfloat16).reshape(NT, MOM, 2, NV, NV)
    spin_sign = jnp.where(jnp.arange(NS) // NV < 2, 1.0, -1.0).astype(jnp.float32)

    def per_pair(operands):
        pair, peramb = operands
        sink = lax.dynamic_index_in_dim(phi, pair[0], 0, keepdims=False)
        source = lax.dynamic_index_in_dim(phi, pair[1], 0, keepdims=False)
        return correlate(sink, source, peramb, spin_sign)
    correlators = lax.map(per_pair, (pairs, perambulators))
    return (elementals, correlators)
```

```python
import functools
import math

import jax
import jax.numpy as jnp
from jax import lax
from jax.experimental import pallas as pl
from jax.experimental.pallas import tpu as pltpu
from jax.sharding import PartitionSpec as P

SPIN = 4
MOM = 4
LX = 16
LY = 16
LZ = 32
ZBLK = 16
MESH = pl.DeviceIdType.MESH
VMEM_LIMIT = 48 * 1024 * 1024


def elementals_kernel(scale, codes, vecs, above, gauge, out, held, wave):
    count, sites = vecs.shape[2], vecs.shape[3]
    plane = above.shape[3]
    lane = lax.broadcasted_iota(jnp.int32, (count, sites), 1)
    ends = {0: lane % LX == LX - 1, 1: (lane // LX) % LY == LY - 1}

    for axis, (near, span) in {0: (1, LX), 1: (LX, plane)}.items():
        used = functools.reduce(jnp.logical_or, [codes[m] // 2 == axis for m in range(MOM)])

        @pl.when(used)
        def _(axis=axis, near=near, span=span):
            for part in range(2):
                for c in range(3):
                    field = vecs[part, c].astype(jnp.float32)
                    inner = pltpu.roll(field, sites - near, 1)
                    outer = pltpu.roll(field, span - near, 1)
                    moved = jnp.where(ends[axis], outer, inner)
                    held[axis, c, pl.ds(part * count, count), :] = moved.astype(jnp.bfloat16)

    for part in range(2):
        for c in range(3):
            rows = pl.ds(part * count, count)
            held[3, c, rows, :] = vecs[part, c]
            held[2, c, rows, pl.ds(0, sites - plane)] = vecs[part, c, :, pl.ds(plane, sites - plane)]
            held[2, c, rows, pl.ds(sites - plane, plane)] = above[part, c]

    for m in range(MOM):
        code = codes[m]
        axis = code // 2
        forward = code % 2 == 0
        source = jnp.where(forward, axis, 3)
        left = jnp.where(forward, 3, axis)
        for start in range(0, sites, 128):
            lanes = pl.ds(start, 128)
            links = [gauge[m, pl.ds(k, 1), lanes] for k in range(18)]

            def rows_step(r, carry, lanes=lanes, links=links):
                row = pl.multiple_of(r * 16, 16)
                fields = [
                    [
                        held[source, b, pl.ds(part * count + row, 16), lanes].astype(jnp.float32)
                        for part in range(2)
                    ]
                    for b in range(3)
                ]
                for c in range(3):
                    real = None
                    imag = None
                    for b in range(3):
                        gr, gi = links[(c * 3 + b) * 2], links[(c * 3 + b) * 2 + 1]
                        xr, xi = fields[b]
                        tr = gr * xr - gi * xi
                        ti = gr * xi + gi * xr
                        real = tr if real is None else real + tr
                        imag = ti if imag is None else imag + ti
                    wave[c, pl.ds(row, 16), lanes] = real.astype(jnp.bfloat16)
                    wave[c, pl.ds(count + row, 16), lanes] = imag.astype(jnp.bfloat16)
                return carry

            lax.fori_loop(0, count // 16, rows_step, 0, unroll=True)
        total = jnp.zeros((2 * count, 2 * count), jnp.float32)
        for c in range(3):
            total = total + lax.dot_general(
                held[left, c],
                wave[c],
                (((1,), (1,)), ((), ())),
                preferred_element_type=jnp.float32,
            )
        real = total[:count, :count] + total[count:, count:]
        imag = total[:count, count:] - total[count:, :count]
        out[m, 0] = (real * scale).astype(jnp.bfloat16)
        out[m, 1] = (imag * scale).astype(jnp.bfloat16)


def exchange_kernel(slab, part, mine, table, landed, held, send, arrive, send_far, send_near, got):
    rows = mine.shape[0]
    groups = slab // ZBLK
    me = lax.axis_index("slab")
    zblock, time = me // groups, me % groups
    own_time = me // ZBLK
    chips = slab // 2
    chip, core = me // 2, me % 2
    partner = chip * 2 + (1 - core)

    barrier = pltpu.get_barrier_semaphore()

    def greet(j, carry):
        pl.semaphore_signal(
            barrier, inc=1, device_id={"slab": lax.rem(me + j, slab)}, device_id_type=MESH
        )
        return carry

    lax.fori_loop(1, slab, greet, 0)
    pl.semaphore_wait(barrier, slab - 1)

    def piece(k):
        return pltpu.make_async_remote_copy(
            src_ref=part.at[pl.ds(pl.multiple_of(k * rows, rows), rows)],
            dst_ref=landed.at[zblock],
            send_sem=send.at[k],
            recv_sem=arrive.at[zblock],
            device_id={"slab": time * ZBLK + k},
            device_id_type=MESH,
        )

    def coming(z):
        return pltpu.make_async_remote_copy(
            src_ref=part.at[pl.ds(0, rows)],
            dst_ref=landed.at[z],
            send_sem=send.at[0],
            recv_sem=arrive.at[z],
            device_id={"slab": partner},
            device_id_type=MESH,
        )

    def send_piece(j, carry):
        k = lax.rem(zblock + j, ZBLK)

        @pl.when(time * ZBLK + k != me)
        def _():
            piece(k).start()

        @pl.when(time * ZBLK + k == me)
        def _():
            landed[zblock] = part[pl.ds(pl.multiple_of(k * rows, rows), rows)]

        return carry

    lax.fori_loop(0, ZBLK, send_piece, 0)

    def take_piece(z, total):
        @pl.when(z * groups + own_time != me)
        def _():
            coming(z).wait_recv()

        return total + landed[z].astype(jnp.float32)

    total = lax.fori_loop(0, ZBLK, take_piece, jnp.zeros(mine.shape, jnp.float32))
    mine[...] = total
    held[me] = total.astype(jnp.bfloat16)

    def block(slot, target, sem):
        return pltpu.make_async_remote_copy(
            src_ref=held.at[slot],
            dst_ref=held.at[slot],
            send_sem=sem,
            recv_sem=got.at[slot],
            device_id={"slab": target},
            device_id_type=MESH,
        )

    block(me, partner, send_near.at[chip]).start()

    def send_far_block(j, carry):
        target = lax.rem(chip + j, chips)
        block(me, target * 2 + core, send_far.at[target]).start()
        return carry

    lax.fori_loop(1, chips, send_far_block, 0)

    def forward(j, carry):
        origin = lax.rem(chip + chips - j, chips)
        slot = origin * 2 + core
        block(slot, partner, send_near.at[origin]).wait_recv()
        block(slot, partner, send_near.at[origin]).start()
        return carry

    lax.fori_loop(1, chips, forward, 0)

    def finish(c, carry):
        block(c * 2 + 1 - core, partner, send_near.at[c]).wait_recv()
        block(c * 2 + core, partner, send_near.at[c]).wait_send()

        @pl.when(c != chip)
        def _():
            block(me, c * 2 + core, send_far.at[c]).wait_send()

        return carry

    lax.fori_loop(0, chips, finish, 0)

    def sent(k, carry):
        @pl.when(time * ZBLK + k != me)
        def _():
            piece(k).wait_send()

        return carry

    lax.fori_loop(0, ZBLK, sent, 0)
    table[...] = held[...]


def correlate_kernel(pairs, phi, tau, out):
    n = pl.program_id(0)
    first, second = pairs[n, 0], pairs[n, 1]
    count = phi.shape[-1]
    size = SPIN * count
    for m in range(MOM):
        fr, fi = phi[first, m, 0], phi[first, m, 1]
        sr, si = phi[second, m, 0], phi[second, m, 1]
        sink = jnp.concatenate(
            [jnp.concatenate([fr, -fi], axis=1), jnp.concatenate([fi, fr], axis=1)], axis=0
        )
        source = jnp.concatenate(
            [jnp.concatenate([sr, si], axis=1), jnp.concatenate([-si, sr], axis=1)], axis=0
        )
        real = jnp.zeros((count, count), jnp.float32)
        imag = jnp.zeros((count, count), jnp.float32)
        for a in range(SPIN):
            rows = slice(a * count, (a + 1) * count)
            stacked = jnp.concatenate([tau[0, 0, rows], tau[0, 1, rows]], axis=0)
            moved = jnp.dot(sink, stacked, preferred_element_type=jnp.float32)
            for b in range(SPIN):
                cols = slice(b * count, (b + 1) * count)
                beside = jnp.concatenate([tau[0, 0, rows, cols], tau[0, 1, rows, cols]], axis=1)
                cross = jnp.dot(beside, source, preferred_element_type=jnp.float32)
                mr, mi = moved[:count, cols], moved[count:, cols]
                cr, ci = cross[:, :count], cross[:, count:]
                tr = mr * cr + mi * ci
                ti = mi * cr - mr * ci
                if (a < 2) == (b < 2):
                    real, imag = real + tr, imag + ti
                else:
                    real, imag = real - tr, imag - ti
        out[n, m, 0] = jnp.sum(real) / size
        out[n, m, 1] = jnp.sum(imag) / size


def phased_links(links, momenta, directions, zblock, depth):
    site_count = links.shape[-1]
    local = jnp.arange(site_count, dtype=jnp.int32)
    axis = directions // 2
    back = directions % 2
    xpos = (local % LX)[None, :] + (back * (axis == 0))[:, None]
    ypos = (local // LX % LY)[None, :] + (back * (axis == 1))[:, None]
    zpos = (local // (LX * LY) + zblock * depth)[None, :] + (back * (axis == 2))[:, None]
    frac = jnp.mod(momenta[:, 0:1] * xpos, LX).astype(jnp.float32) / LX
    frac = frac + jnp.mod(momenta[:, 1:2] * ypos, LY).astype(jnp.float32) / LY
    frac = frac + jnp.mod(momenta[:, 2:3] * zpos, LZ).astype(jnp.float32) / LZ
    angle = 2.0 * math.pi * frac
    cosine, sine = jnp.cos(angle)[:, None, None], jnp.sin(angle)[:, None, None]
    field = links.astype(jnp.float32)
    a = axis[:, None, None, None]
    chosen = [
        jnp.where(a == 0, field[0, p], jnp.where(a == 1, field[1, p], field[2, p]))
        for p in range(2)
    ]
    adjoint = (back == 1)[:, None, None, None]
    real = jnp.where(adjoint, jnp.swapaxes(chosen[0], 1, 2), chosen[0])
    imag = jnp.where(adjoint, -jnp.swapaxes(chosen[1], 1, 2), chosen[1])
    both = jnp.stack([real * cosine + imag * sine, imag * cosine - real * sine], axis=3)
    return both.reshape(directions.shape[0], 18, site_count)


def on_device(eigvecs, links, momenta, directions, pairs, perambulators):
    count = eigvecs.shape[3]
    site_count = eigvecs.shape[4]
    slab = lax.axis_size("slab")
    groups = slab // ZBLK
    plane = LX * LY
    position = lax.axis_index("slab")
    route = [((i + groups) % slab, i) for i in range(slab)]
    above = lax.ppermute(eigvecs[0, ..., :plane], "slab", route)
    gauge = phased_links(links[0], momenta, directions, position // groups, site_count // plane)
    scale = 1.0 / math.sqrt(3.0 * site_count * ZBLK)
    vmem = pl.BlockSpec(memory_space=pltpu.VMEM)
    smem = pl.BlockSpec(memory_space=pltpu.SMEM)
    part = pl.pallas_call(
        functools.partial(elementals_kernel, scale),
        out_shape=jax.ShapeDtypeStruct((MOM, 2, count, count), jnp.bfloat16),
        in_specs=[smem, vmem, vmem, vmem],
        out_specs=vmem,
        scratch_shapes=[
            pltpu.VMEM((4, 3, 2 * count, site_count), jnp.bfloat16),
            pltpu.VMEM((3, 2 * count, site_count), jnp.bfloat16),
        ],
        compiler_params=pltpu.CompilerParams(vmem_limit_bytes=VMEM_LIMIT),
        name="elementals",
    )(directions, eigvecs[0], above, gauge)
    part = part.reshape(MOM * 2 * count, count)
    share = part.shape[0] // ZBLK
    mine, table = pl.pallas_call(
        functools.partial(exchange_kernel, slab),
        out_shape=(
            jax.ShapeDtypeStruct((share, count), jnp.float32),
            jax.ShapeDtypeStruct((slab, share, count), jnp.bfloat16),
        ),
        in_specs=[vmem],
        out_specs=(vmem, vmem),
        scratch_shapes=[
            pltpu.VMEM((ZBLK, share, count), jnp.bfloat16),
            pltpu.VMEM((slab, share, count), jnp.bfloat16),
            pltpu.SemaphoreType.DMA((ZBLK,)),
            pltpu.SemaphoreType.DMA((ZBLK,)),
            pltpu.SemaphoreType.DMA((slab // 2,)),
            pltpu.SemaphoreType.DMA((slab // 2,)),
            pltpu.SemaphoreType.DMA((slab,)),
        ],
        compiler_params=pltpu.CompilerParams(
            collective_id=0, has_side_effects=True, vmem_limit_bytes=VMEM_LIMIT
        ),
        name="exchange",
    )(part)
    phi = table.reshape(groups, MOM, 2, count, count)
    correlators = pl.pallas_call(
        correlate_kernel,
        grid=(pairs.shape[0],),
        out_shape=jax.ShapeDtypeStruct((pairs.shape[0], MOM, 2), jnp.float32),
        in_specs=[
            smem,
            vmem,
            pl.BlockSpec((1,) + perambulators.shape[1:], lambda n: (n, 0, 0, 0)),
        ],
        out_specs=smem,
        compiler_params=pltpu.CompilerParams(vmem_limit_bytes=VMEM_LIMIT),
        name="correlate",
    )(pairs, phi, perambulators)
    return (mine, correlators)


def solution(mesh):
    return jax.shard_map(
        on_device,
        mesh=mesh,
        in_specs=(
            P(("groups", "slab"), None, None, None, None),
            P(("groups", "slab"), None, None, None, None, None),
            P(),
            P(),
            P(("groups", "slab"), None),
            P(("groups", "slab"), None, None, None),
        ),
        out_specs=(P(("groups", "slab"), None), P(("groups", "slab"), None, None)),
        check_vma=False,
    )
```

```python
import functools
import math

import jax
import jax.numpy as jnp
from jax import lax
from jax.experimental import pallas as pl
from jax.experimental.pallas import tpu as pltpu
from jax.sharding import PartitionSpec as P

SPIN = 4
MOM = 4
LX = 16
LY = 16
LZ = 32
ZBLK = 16
MESH = pl.DeviceIdType.MESH
VMEM_LIMIT = 48 * 1024 * 1024


def displace(gauge, field, left, wave, m, lanes_from, lanes_to, count, shift):
    for start in range(lanes_from, lanes_to, 128):
        lanes = pl.ds(start, 128)
        near = pl.ds(start - shift, 128)
        links = [gauge[m, pl.ds(k, 1), lanes] for k in range(18)]

        def rows_step(r, carry, near=near, links=links):
            row = pl.multiple_of(r * 16, 16)
            fields = [
                [field(b, pl.ds(part * count + row, 16), near) for part in range(2)]
                for b in range(3)
            ]
            for c in range(3):
                real = None
                imag = None
                for b in range(3):
                    gr, gi = links[(c * 3 + b) * 2], links[(c * 3 + b) * 2 + 1]
                    xr, xi = fields[b]
                    tr = gr * xr - gi * xi
                    ti = gr * xi + gi * xr
                    real = tr if real is None else real + tr
                    imag = ti if imag is None else imag + ti
                wave[c, pl.ds(row, 16), near] = real.astype(jnp.bfloat16)
                wave[c, pl.ds(count + row, 16), near] = imag.astype(jnp.bfloat16)
            return carry

        lax.fori_loop(0, count // 16, rows_step, 0, unroll=True)
    whole = pl.ds(lanes_from - shift, lanes_to - lanes_from)
    total = None
    for c in range(3):
        term = lax.dot_general(
            left(c, whole),
            wave[c, :, whole],
            (((1,), (1,)), ((), ())),
            preferred_element_type=jnp.float32,
        )
        total = term if total is None else total + term
    return total


def local_kernel(plane, codes, vecs, gauge, out, held, wave):
    count, sites = vecs.shape[2], vecs.shape[3]
    lane = lax.broadcasted_iota(jnp.int32, (count, sites), 1)
    ends = {0: lane % LX == LX - 1, 1: (lane // LX) % LY == LY - 1}

    for axis, (near, span) in {0: (1, LX), 1: (LX, plane)}.items():
        used = functools.reduce(jnp.logical_or, [codes[m] // 2 == axis for m in range(MOM)])

        @pl.when(used)
        def _(axis=axis, near=near, span=span):
            for part in range(2):
                for c in range(3):
                    field = vecs[part, c].astype(jnp.float32)
                    inner = pltpu.roll(field, sites - near, 1)
                    outer = pltpu.roll(field, span - near, 1)
                    moved = jnp.where(ends[axis], outer, inner)
                    held[axis, c, pl.ds(part * count, count), :] = moved.astype(jnp.bfloat16)

    for part in range(2):
        for c in range(3):
            rows = pl.ds(part * count, count)
            held[3, c, rows, :] = vecs[part, c]
            held[2, c, rows, pl.ds(0, sites - plane)] = vecs[part, c, :, pl.ds(plane, sites - plane)]

    for m in range(MOM):
        axis = codes[m] // 2
        forward = codes[m] % 2 == 0
        source = jnp.where(forward, axis, 3)
        left = jnp.where(forward, 3, axis)

        def run(first, last, m=m, source=source, left=left):
            return displace(
                gauge,
                lambda b, rows, lanes: held[source, b, rows, lanes].astype(jnp.float32),
                lambda c, lanes: held[left, c, :, lanes],
                wave,
                m,
                first,
                last,
                count,
                0,
            )

        @pl.when(axis == 2)
        def _(m=m, run=run):
            out[m] = run(0, sites - plane)

        @pl.when(axis != 2)
        def _(m=m, run=run):
            out[m] = run(0, sites)


def border_kernel(scale, codes, vecs, above, gauge, inner, out, held, wave):
    count, sites = vecs.shape[2], vecs.shape[3]
    plane = above.shape[3]
    for part in range(2):
        for c in range(3):
            rows = pl.ds(part * count, count)
            held[0, c, rows, :] = vecs[part, c, :, pl.ds(sites - plane, plane)]
            held[1, c, rows, :] = above[part, c]

    def put(m, total):
        real = total[:count, :count] + total[count:, count:]
        imag = total[:count, count:] - total[count:, :count]
        out[m, 0] = (real * scale).astype(jnp.bfloat16)
        out[m, 1] = (imag * scale).astype(jnp.bfloat16)

    for m in range(MOM):
        axis = codes[m] // 2
        forward = codes[m] % 2 == 0
        source = jnp.where(forward, 1, 0)

        @pl.when(axis == 2)
        def _(m=m, source=source):
            total = displace(
                gauge,
                lambda b, rows, lanes: held[source, b, rows, lanes].astype(jnp.float32),
                lambda c, lanes: held[1 - source, c, :, lanes],
                wave,
                m,
                sites - plane,
                sites,
                count,
                sites - plane,
            )
            put(m, inner[m] + total)

        @pl.when(axis != 2)
        def _(m=m):
            put(m, inner[m])


def exchange_kernel(slab, part, mine, table, landed, held, send, arrive, send_far, send_near, got):
    rows = mine.shape[0]
    groups = slab // ZBLK
    me = lax.axis_index("slab")
    zblock, time = me // groups, me % groups
    own_time = me // ZBLK
    chips = slab // 2
    chip, core = me // 2, me % 2
    partner = chip * 2 + (1 - core)

    barrier = pltpu.get_barrier_semaphore()

    def greet(j, carry):
        pl.semaphore_signal(
            barrier, inc=1, device_id={"slab": lax.rem(me + j, slab)}, device_id_type=MESH
        )
        return carry

    lax.fori_loop(1, slab, greet, 0)
    pl.semaphore_wait(barrier, slab - 1)

    def piece(k):
        return pltpu.make_async_remote_copy(
            src_ref=part.at[pl.ds(pl.multiple_of(k * rows, rows), rows)],
            dst_ref=landed.at[zblock],
            send_sem=send.at[k],
            recv_sem=arrive.at[zblock],
            device_id={"slab": time * ZBLK + k},
            device_id_type=MESH,
        )

    def coming(z):
        return pltpu.make_async_remote_copy(
            src_ref=part.at[pl.ds(0, rows)],
            dst_ref=landed.at[z],
            send_sem=send.at[0],
            recv_sem=arrive.at[z],
            device_id={"slab": partner},
            device_id_type=MESH,
        )

    def send_piece(j, carry):
        k = lax.rem(zblock + j, ZBLK)

        @pl.when(time * ZBLK + k != me)
        def _():
            piece(k).start()

        @pl.when(time * ZBLK + k == me)
        def _():
            landed[zblock] = part[pl.ds(pl.multiple_of(k * rows, rows), rows)]

        return carry

    lax.fori_loop(0, ZBLK, send_piece, 0)

    def take_piece(z, total):
        @pl.when(z * groups + own_time != me)
        def _():
            coming(z).wait_recv()

        return total + landed[z].astype(jnp.float32)

    total = lax.fori_loop(0, ZBLK, take_piece, jnp.zeros(mine.shape, jnp.float32))
    mine[...] = total
    held[me] = total.astype(jnp.bfloat16)

    def block(slot, target, sem):
        return pltpu.make_async_remote_copy(
            src_ref=held.at[slot],
            dst_ref=held.at[slot],
            send_sem=sem,
            recv_sem=got.at[slot],
            device_id={"slab": target},
            device_id_type=MESH,
        )

    block(me, partner, send_near.at[chip]).start()

    def send_far_block(j, carry):
        target = lax.rem(chip + j, chips)
        block(me, target * 2 + core, send_far.at[target]).start()
        return carry

    lax.fori_loop(1, chips, send_far_block, 0)

    def forward(j, carry):
        origin = lax.rem(chip + chips - j, chips)
        slot = origin * 2 + core
        block(slot, partner, send_near.at[origin]).wait_recv()
        block(slot, partner, send_near.at[origin]).start()
        return carry

    lax.fori_loop(1, chips, forward, 0)

    def finish(c, carry):
        block(c * 2 + 1 - core, partner, send_near.at[c]).wait_recv()
        block(c * 2 + core, partner, send_near.at[c]).wait_send()

        @pl.when(c != chip)
        def _():
            block(me, c * 2 + core, send_far.at[c]).wait_send()

        return carry

    lax.fori_loop(0, chips, finish, 0)

    def sent(k, carry):
        @pl.when(time * ZBLK + k != me)
        def _():
            piece(k).wait_send()

        return carry

    lax.fori_loop(0, ZBLK, sent, 0)
    table[...] = held[...]


def correlate_kernel(pairs, phi, tau, mine, out, rows_out):
    n = pl.program_id(0)
    first, second = pairs[n, 0], pairs[n, 1]
    count = phi.shape[-1]
    size = SPIN * count
    rows_out[...] = mine[...]
    row = lax.broadcasted_iota(jnp.int32, (2, MOM), 1)
    part = lax.broadcasted_iota(jnp.int32, (2, MOM), 0)
    values = jnp.zeros((2, MOM), jnp.float32)
    for m in range(MOM):
        fr, fi = phi[first, m, 0], phi[first, m, 1]
        sr, si = phi[second, m, 0], phi[second, m, 1]
        sink = jnp.concatenate(
            [jnp.concatenate([fr, -fi], axis=1), jnp.concatenate([fi, fr], axis=1)], axis=0
        )
        source = jnp.concatenate(
            [jnp.concatenate([sr, si], axis=1), jnp.concatenate([-si, sr], axis=1)], axis=0
        )
        real = jnp.zeros((count, count), jnp.float32)
        imag = jnp.zeros((count, count), jnp.float32)
        for a in range(SPIN):
            rows = slice(a * count, (a + 1) * count)
            stacked = jnp.concatenate([tau[0, 0, rows], tau[0, 1, rows]], axis=0)
            moved = jnp.dot(sink, stacked, preferred_element_type=jnp.float32)
            for b in range(SPIN):
                cols = slice(b * count, (b + 1) * count)
                beside = jnp.concatenate([tau[0, 0, rows, cols], tau[0, 1, rows, cols]], axis=1)
                cross = jnp.dot(beside, source, preferred_element_type=jnp.float32)
                mr, mi = moved[:count, cols], moved[count:, cols]
                cr, ci = cross[:, :count], cross[:, count:]
                tr = mr * cr + mi * ci
                ti = mi * cr - mr * ci
                if (a < 2) == (b < 2):
                    real, imag = real + tr, imag + ti
                else:
                    real, imag = real - tr, imag - ti
        both = jnp.where(part == 0, jnp.sum(real), jnp.sum(imag)) / size
        values = jnp.where(row == m, both, values)
    out[n] = values


def phased_links(links, momenta, directions, zblock, depth):
    site_count = links.shape[-1]
    local = jnp.arange(site_count, dtype=jnp.int32)
    axis = directions // 2
    back = directions % 2
    xpos = (local % LX)[None, :] + (back * (axis == 0))[:, None]
    ypos = (local // LX % LY)[None, :] + (back * (axis == 1))[:, None]
    zpos = (local // (LX * LY) + zblock * depth)[None, :] + (back * (axis == 2))[:, None]
    frac = jnp.mod(momenta[:, 0:1] * xpos, LX).astype(jnp.float32) / LX
    frac = frac + jnp.mod(momenta[:, 1:2] * ypos, LY).astype(jnp.float32) / LY
    frac = frac + jnp.mod(momenta[:, 2:3] * zpos, LZ).astype(jnp.float32) / LZ
    angle = 2.0 * math.pi * frac
    cosine, sine = jnp.cos(angle)[:, None, None], jnp.sin(angle)[:, None, None]
    field = links.astype(jnp.float32)
    a = axis[:, None, None, None]
    chosen = [
        jnp.where(a == 0, field[0, p], jnp.where(a == 1, field[1, p], field[2, p]))
        for p in range(2)
    ]
    adjoint = (back == 1)[:, None, None, None]
    real = jnp.where(adjoint, jnp.swapaxes(chosen[0], 1, 2), chosen[0])
    imag = jnp.where(adjoint, -jnp.swapaxes(chosen[1], 1, 2), chosen[1])
    both = jnp.stack([real * cosine + imag * sine, imag * cosine - real * sine], axis=3)
    return both.reshape(directions.shape[0], 18, site_count)


def on_device(eigvecs, links, momenta, directions, pairs, perambulators):
    count = eigvecs.shape[3]
    site_count = eigvecs.shape[4]
    slab = lax.axis_size("slab")
    groups = slab // ZBLK
    plane = LX * LY
    position = lax.axis_index("slab")
    route = [((i + groups) % slab, i) for i in range(slab)]
    above = lax.ppermute(eigvecs[0, ..., :plane], "slab", route)
    gauge = phased_links(links[0], momenta, directions, position // groups, site_count // plane)
    scale = 1.0 / math.sqrt(3.0 * site_count * ZBLK)
    vmem = pl.BlockSpec(memory_space=pltpu.VMEM)
    smem = pl.BlockSpec(memory_space=pltpu.SMEM)
    inner = pl.pallas_call(
        functools.partial(local_kernel, plane),
        out_shape=jax.ShapeDtypeStruct((MOM, 2 * count, 2 * count), jnp.float32),
        in_specs=[smem, vmem, vmem],
        out_specs=vmem,
        scratch_shapes=[
            pltpu.VMEM((4, 3, 2 * count, site_count), jnp.bfloat16),
            pltpu.VMEM((3, 2 * count, site_count), jnp.bfloat16),
        ],
        compiler_params=pltpu.CompilerParams(vmem_limit_bytes=VMEM_LIMIT),
        cost_estimate=pl.CostEstimate(
            flops=MOM * 8 * count * count * 3 * site_count,
            bytes_accessed=12 * count * site_count,
            transcendentals=0,
        ),
        name="local",
    )(directions, eigvecs[0], gauge)
    part = pl.pallas_call(
        functools.partial(border_kernel, scale),
        out_shape=jax.ShapeDtypeStruct((MOM, 2, count, count), jnp.bfloat16),
        in_specs=[smem, vmem, vmem, vmem, vmem],
        out_specs=vmem,
        scratch_shapes=[
            pltpu.VMEM((2, 3, 2 * count, plane), jnp.bfloat16),
            pltpu.VMEM((3, 2 * count, plane), jnp.bfloat16),
        ],
        compiler_params=pltpu.CompilerParams(vmem_limit_bytes=VMEM_LIMIT),
        name="border",
    )(directions, eigvecs[0], above, gauge, inner)
    part = part.reshape(MOM * 2 * count, count)
    share = part.shape[0] // ZBLK
    mine, table = pl.pallas_call(
        functools.partial(exchange_kernel, slab),
        out_shape=(
            jax.ShapeDtypeStruct((share, count), jnp.float32),
            jax.ShapeDtypeStruct((slab, share, count), jnp.bfloat16),
        ),
        in_specs=[vmem],
        out_specs=(vmem, vmem),
        scratch_shapes=[
            pltpu.VMEM((ZBLK, share, count), jnp.bfloat16),
            pltpu.VMEM((slab, share, count), jnp.bfloat16),
            pltpu.SemaphoreType.DMA((ZBLK,)),
            pltpu.SemaphoreType.DMA((ZBLK,)),
            pltpu.SemaphoreType.DMA((slab // 2,)),
            pltpu.SemaphoreType.DMA((slab // 2,)),
            pltpu.SemaphoreType.DMA((slab,)),
        ],
        compiler_params=pltpu.CompilerParams(
            collective_id=0, has_side_effects=True, vmem_limit_bytes=VMEM_LIMIT
        ),
        name="exchange",
    )(part)
    phi = table.reshape(groups, MOM, 2, count, count)
    correlators, mine = pl.pallas_call(
        correlate_kernel,
        grid=(pairs.shape[0],),
        out_shape=(
            jax.ShapeDtypeStruct((pairs.shape[0], 2, MOM), jnp.float32),
            jax.ShapeDtypeStruct((share, count), jnp.float32),
        ),
        in_specs=[
            smem,
            vmem,
            pl.BlockSpec((1,) + perambulators.shape[1:], lambda n: (n, 0, 0, 0)),
            vmem,
        ],
        out_specs=(vmem, vmem),
        compiler_params=pltpu.CompilerParams(vmem_limit_bytes=VMEM_LIMIT),
        name="correlate",
    )(jnp.clip(pairs, 0, groups - 1), phi, perambulators, mine)
    return (mine, jnp.swapaxes(correlators, 1, 2))


def solution(mesh):
    return jax.shard_map(
        on_device,
        mesh=mesh,
        in_specs=(
            P(("groups", "slab"), None, None, None, None),
            P(("groups", "slab"), None, None, None, None, None),
            P(),
            P(),
            P(("groups", "slab"), None),
            P(("groups", "slab"), None, None, None),
        ),
        out_specs=(P(("groups", "slab"), None), P(("groups", "slab"), None, None)),
        check_vma=False,
    )
```

```python
import functools
import math

import jax
import jax.numpy as jnp
from jax import lax
from jax.experimental import pallas as pl
from jax.experimental.pallas import tpu as pltpu
from jax.sharding import PartitionSpec as P

SPIN = 4
MOM = 4
LX = 16
LY = 16
LZ = 32
ZBLK = 16
MESH = pl.DeviceIdType.MESH
VMEM_LIMIT = 48 * 1024 * 1024


def displace(gauge, field, left, wave, m, lanes_from, lanes_to, count, shift):
    for start in range(lanes_from, lanes_to, 128):
        lanes = pl.ds(start, 128)
        near = pl.ds(start - shift, 128)
        links = [gauge[m, pl.ds(k, 1), lanes] for k in range(18)]

        def rows_step(r, carry, near=near, links=links):
            row = pl.multiple_of(r * 16, 16)
            fields = [
                [field(part, b, row, near).astype(jnp.float32) for part in range(2)]
                for b in range(3)
            ]
            for c in range(3):
                real = None
                imag = None
                for b in range(3):
                    gr, gi = links[(c * 3 + b) * 2], links[(c * 3 + b) * 2 + 1]
                    xr, xi = fields[b]
                    tr = gr * xr - gi * xi
                    ti = gr * xi + gi * xr
                    real = tr if real is None else real + tr
                    imag = ti if imag is None else imag + ti
                wave[c, pl.ds(row, 16), near] = real.astype(jnp.bfloat16)
                wave[c, pl.ds(count + row, 16), near] = imag.astype(jnp.bfloat16)
            return carry

        lax.fori_loop(0, count // 16, rows_step, 0, unroll=True)
    whole = pl.ds(lanes_from - shift, lanes_to - lanes_from)
    total = None
    for c in range(3):
        term = lax.dot_general(
            left(c, whole),
            wave[c, :, whole],
            (((1,), (1,)), ((), ())),
            preferred_element_type=jnp.float32,
        )
        total = term if total is None else total + term
    return total


def local_kernel(plane, codes, vecs, gauge, out, held, wave):
    count, sites = vecs.shape[2], vecs.shape[3]
    lane = lax.broadcasted_iota(jnp.int32, (count, sites), 1)
    ends = {0: lane % LX == LX - 1, 1: (lane // LX) % LY == LY - 1}

    for axis, (near, span) in {0: (1, LX), 1: (LX, plane)}.items():
        used = functools.reduce(jnp.logical_or, [codes[m] // 2 == axis for m in range(MOM)])

        @pl.when(used)
        def _(axis=axis, near=near, span=span):
            for part in range(2):
                for c in range(3):
                    field = vecs[part, c].astype(jnp.float32)
                    inner = pltpu.roll(field, sites - near, 1)
                    outer = pltpu.roll(field, span - near, 1)
                    moved = jnp.where(ends[axis], outer, inner)
                    held[axis, c, pl.ds(part * count, count), :] = moved.astype(jnp.bfloat16)

    for part in range(2):
        for c in range(3):
            rows = pl.ds(part * count, count)
            held[3, c, rows, :] = vecs[part, c]
            held[2, c, rows, pl.ds(0, sites - plane)] = vecs[part, c, :, pl.ds(plane, sites - plane)]

    for m in range(MOM):
        axis = codes[m] // 2
        forward = codes[m] % 2 == 0
        source = jnp.where(forward, axis, 3)
        left = jnp.where(forward, 3, axis)

        def run(first, last, m=m, source=source, left=left):
            return displace(
                gauge,
                lambda part, b, row, lanes: held[source, b, pl.ds(part * count + row, 16), lanes],
                lambda c, lanes: held[left, c, :, lanes],
                wave,
                m,
                first,
                last,
                count,
                0,
            )

        @pl.when(axis == 2)
        def _(m=m, run=run):
            out[m] = run(0, sites - plane)

        @pl.when(axis != 2)
        def _(m=m, run=run):
            out[m] = run(0, sites)


def border_kernel(scale, codes, vecs, above, gauge, inner, out, wave):
    count, sites = vecs.shape[2], vecs.shape[3]
    plane = above.shape[3]
    depth = sites - plane
    top = vecs.at[:, :, :, pl.ds(depth, plane)]

    def put(m, total):
        real = total[:count, :count] + total[count:, count:]
        imag = total[:count, count:] - total[count:, :count]
        out[m, 0] = (real * scale).astype(jnp.bfloat16)
        out[m, 1] = (imag * scale).astype(jnp.bfloat16)

    def step(m, moved, left):
        total = displace(
            gauge,
            lambda part, b, row, lanes: moved[part, b, pl.ds(row, 16), lanes],
            lambda c, lanes: jnp.concatenate([left[0, c, :, lanes], left[1, c, :, lanes]], axis=0),
            wave,
            m,
            depth,
            sites,
            count,
            depth,
        )
        put(m, inner[m] + total)

    for m in range(MOM):
        axis = codes[m] // 2
        forward = codes[m] % 2 == 0

        @pl.when(jnp.logical_and(axis == 2, forward))
        def _(m=m):
            step(m, above, top)

        @pl.when(jnp.logical_and(axis == 2, jnp.logical_not(forward)))
        def _(m=m):
            step(m, top, above)

        @pl.when(axis != 2)
        def _(m=m):
            put(m, inner[m])


def exchange_kernel(slab, part, mine, table, landed, held, send, arrive, send_far, send_near, got):
    rows = mine.shape[0]
    groups = slab // ZBLK
    me = lax.axis_index("slab")
    zblock, time = me // groups, me % groups
    own_time = me // ZBLK

    barrier = pltpu.get_barrier_semaphore()

    def greet(j, carry):
        source = lax.rem(zblock + j, ZBLK) * groups + own_time

        @pl.when(source != me)
        def _():
            pl.semaphore_signal(barrier, inc=1, device_id={"slab": source}, device_id_type=MESH)

        return carry

    lax.fori_loop(0, ZBLK, greet, 0)

    def mate(j):
        return zblock * groups + lax.rem(time + j, groups)

    for j in range(1, groups):
        pl.semaphore_signal(barrier, inc=1, device_id={"slab": mate(j)}, device_id_type=MESH)
    pl.semaphore_wait(barrier, jnp.where(own_time == time, ZBLK - 1, ZBLK) + groups - 1)

    def piece(k):
        return pltpu.make_async_remote_copy(
            src_ref=part.at[pl.ds(pl.multiple_of(k * rows, rows), rows)],
            dst_ref=landed.at[zblock],
            send_sem=send.at[k],
            recv_sem=arrive.at[zblock],
            device_id={"slab": time * ZBLK + k},
            device_id_type=MESH,
        )

    def coming(z):
        return pltpu.make_async_remote_copy(
            src_ref=part.at[pl.ds(0, rows)],
            dst_ref=landed.at[z],
            send_sem=send.at[0],
            recv_sem=arrive.at[z],
            device_id={"slab": lax.rem(me + 1, slab)},
            device_id_type=MESH,
        )

    def send_piece(j, carry):
        k = lax.rem(zblock + j, ZBLK)

        @pl.when(time * ZBLK + k != me)
        def _():
            piece(k).start()

        @pl.when(time * ZBLK + k == me)
        def _():
            landed[zblock] = part[pl.ds(pl.multiple_of(k * rows, rows), rows)]

        return carry

    lax.fori_loop(0, ZBLK, send_piece, 0)

    def take_piece(z, total):
        @pl.when(z * groups + own_time != me)
        def _():
            coming(z).wait_recv()

        return total + landed[z].astype(jnp.float32)

    total = lax.fori_loop(0, ZBLK, take_piece, jnp.zeros(mine.shape, jnp.float32))
    mine[...] = total
    held[me] = total.astype(jnp.bfloat16)

    def block(slot, target, sem):
        return pltpu.make_async_remote_copy(
            src_ref=held.at[slot],
            dst_ref=held.at[slot],
            send_sem=sem,
            recv_sem=got.at[slot],
            device_id={"slab": target},
            device_id_type=MESH,
        )

    def send_far_block(j, carry):
        z = lax.rem(zblock + j, ZBLK)
        target = z * groups + own_time

        @pl.when(target != me)
        def _():
            block(me, target, send_far.at[z]).start()

        return carry

    lax.fori_loop(0, ZBLK, send_far_block, 0)

    def forward(j, carry):
        k = lax.rem(me + j, ZBLK)
        slot = time * ZBLK + k

        @pl.when(slot != me)
        def _():
            block(slot, mate(1), send_near.at[k]).wait_recv()

        for i in range(1, groups):

            @pl.when(slot != mate(i))
            def _(i=i):
                block(slot, mate(i), send_near.at[(i - 1) * ZBLK + k]).start()

        return carry

    lax.fori_loop(0, ZBLK, forward, 0)

    def finish(k, carry):
        for i in range(1, groups):
            origin = lax.rem(time + groups - i, groups)

            @pl.when(origin * ZBLK + k != me)
            def _(origin=origin):
                block(origin * ZBLK + k, mate(1), send_near.at[k]).wait_recv()

        for i in range(1, groups):

            @pl.when(time * ZBLK + k != mate(i))
            def _(i=i):
                block(time * ZBLK + k, mate(i), send_near.at[(i - 1) * ZBLK + k]).wait_send()

        @pl.when(k * groups + own_time != me)
        def _():
            block(me, k * groups + own_time, send_far.at[k]).wait_send()

        return carry

    lax.fori_loop(0, ZBLK, finish, 0)

    def sent(k, carry):
        @pl.when(time * ZBLK + k != me)
        def _():
            piece(k).wait_send()

        return carry

    lax.fori_loop(0, ZBLK, sent, 0)
    table[...] = held[...]


def correlate_kernel(pairs, phi, tau, mine, out, rows_out):
    n = pl.program_id(0)
    first, second = pairs[n, 0], pairs[n, 1]
    count = phi.shape[-1]
    size = SPIN * count
    rows_out[...] = mine[...]
    row = lax.broadcasted_iota(jnp.int32, (2, MOM), 1)
    part = lax.broadcasted_iota(jnp.int32, (2, MOM), 0)
    values = jnp.zeros((2, MOM), jnp.float32)
    for m in range(MOM):
        fr, fi = phi[first, m, 0], phi[first, m, 1]
        sr, si = phi[second, m, 0], phi[second, m, 1]
        sink = jnp.concatenate(
            [jnp.concatenate([fr, -fi], axis=1), jnp.concatenate([fi, fr], axis=1)], axis=0
        )
        source = jnp.concatenate(
            [jnp.concatenate([sr, si], axis=1), jnp.concatenate([-si, sr], axis=1)], axis=0
        )
        real = jnp.zeros((count, count), jnp.float32)
        imag = jnp.zeros((count, count), jnp.float32)
        for a in range(SPIN):
            rows = slice(a * count, (a + 1) * count)
            stacked = jnp.concatenate([tau[0, 0, rows], tau[0, 1, rows]], axis=0)
            moved = jnp.dot(sink, stacked, preferred_element_type=jnp.float32)
            for b in range(SPIN):
                cols = slice(b * count, (b + 1) * count)
                beside = jnp.concatenate([tau[0, 0, rows, cols], tau[0, 1, rows, cols]], axis=1)
                cross = jnp.dot(beside, source, preferred_element_type=jnp.float32)
                mr, mi = moved[:count, cols], moved[count:, cols]
                cr, ci = cross[:, :count], cross[:, count:]
                tr = mr * cr + mi * ci
                ti = mi * cr - mr * ci
                if (a < 2) == (b < 2):
                    real, imag = real + tr, imag + ti
                else:
                    real, imag = real - tr, imag - ti
        both = jnp.where(part == 0, jnp.sum(real), jnp.sum(imag)) / size
        values = jnp.where(row == m, both, values)
    out[n] = values


def phased_links(links, momenta, directions, zblock, depth):
    site_count = links.shape[-1]
    local = jnp.arange(site_count, dtype=jnp.int32)
    axis = directions // 2
    back = directions % 2
    xpos = (local % LX)[None, :] + (back * (axis == 0))[:, None]
    ypos = (local // LX % LY)[None, :] + (back * (axis == 1))[:, None]
    zpos = (local // (LX * LY) + zblock * depth)[None, :] + (back * (axis == 2))[:, None]
    frac = jnp.mod(momenta[:, 0:1] * xpos, LX).astype(jnp.float32) / LX
    frac = frac + jnp.mod(momenta[:, 1:2] * ypos, LY).astype(jnp.float32) / LY
    frac = frac + jnp.mod(momenta[:, 2:3] * zpos, LZ).astype(jnp.float32) / LZ
    angle = 2.0 * math.pi * frac
    cosine, sine = jnp.cos(angle)[:, None, None], jnp.sin(angle)[:, None, None]
    field = links.astype(jnp.float32)
    a = axis[:, None, None, None]
    chosen = [
        jnp.where(a == 0, field[0, p], jnp.where(a == 1, field[1, p], field[2, p]))
        for p in range(2)
    ]
    adjoint = (back == 1)[:, None, None, None]
    real = jnp.where(adjoint, jnp.swapaxes(chosen[0], 1, 2), chosen[0])
    imag = jnp.where(adjoint, -jnp.swapaxes(chosen[1], 1, 2), chosen[1])
    both = jnp.stack([real * cosine + imag * sine, imag * cosine - real * sine], axis=3)
    return both.reshape(directions.shape[0], 18, site_count)


def on_device(eigvecs, links, momenta, directions, pairs, perambulators):
    count = eigvecs.shape[3]
    site_count = eigvecs.shape[4]
    slab = lax.axis_size("slab")
    groups = slab // ZBLK
    plane = LX * LY
    position = lax.axis_index("slab")
    route = [((i + groups) % slab, i) for i in range(slab)]
    above = lax.ppermute(eigvecs[0, ..., :plane], "slab", route)
    gauge = phased_links(links[0], momenta, directions, position // groups, site_count // plane)
    scale = 1.0 / math.sqrt(3.0 * site_count * ZBLK)
    vmem = pl.BlockSpec(memory_space=pltpu.VMEM)
    smem = pl.BlockSpec(memory_space=pltpu.SMEM)
    inner = pl.pallas_call(
        functools.partial(local_kernel, plane),
        out_shape=jax.ShapeDtypeStruct((MOM, 2 * count, 2 * count), jnp.float32),
        in_specs=[smem, vmem, vmem],
        out_specs=vmem,
        scratch_shapes=[
            pltpu.VMEM((4, 3, 2 * count, site_count), jnp.bfloat16),
            pltpu.VMEM((3, 2 * count, site_count), jnp.bfloat16),
        ],
        compiler_params=pltpu.CompilerParams(vmem_limit_bytes=VMEM_LIMIT),
        cost_estimate=pl.CostEstimate(
            flops=MOM * 8 * count * count * 3 * site_count,
            bytes_accessed=12 * count * site_count,
            transcendentals=0,
        ),
        name="local",
    )(directions, eigvecs[0], gauge)
    part = pl.pallas_call(
        functools.partial(border_kernel, scale),
        out_shape=jax.ShapeDtypeStruct((MOM, 2, count, count), jnp.bfloat16),
        in_specs=[smem, vmem, vmem, vmem, vmem],
        out_specs=vmem,
        scratch_shapes=[
            pltpu.VMEM((3, 2 * count, plane), jnp.bfloat16),
        ],
        compiler_params=pltpu.CompilerParams(vmem_limit_bytes=VMEM_LIMIT),
        name="border",
    )(directions, eigvecs[0], above, gauge, inner)
    part = part.reshape(MOM * 2 * count, count)
    share = part.shape[0] // ZBLK
    mine, table = pl.pallas_call(
        functools.partial(exchange_kernel, slab),
        out_shape=(
            jax.ShapeDtypeStruct((share, count), jnp.float32),
            jax.ShapeDtypeStruct((slab, share, count), jnp.bfloat16),
        ),
        in_specs=[vmem],
        out_specs=(vmem, vmem),
        scratch_shapes=[
            pltpu.VMEM((ZBLK, share, count), jnp.bfloat16),
            pltpu.VMEM((slab, share, count), jnp.bfloat16),
            pltpu.SemaphoreType.DMA((ZBLK,)),
            pltpu.SemaphoreType.DMA((ZBLK,)),
            pltpu.SemaphoreType.DMA((ZBLK,)),
            pltpu.SemaphoreType.DMA(((groups - 1) * ZBLK,)),
            pltpu.SemaphoreType.DMA((slab,)),
        ],
        compiler_params=pltpu.CompilerParams(
            collective_id=0, has_side_effects=True, vmem_limit_bytes=VMEM_LIMIT
        ),
        name="exchange",
    )(part)
    phi = table.reshape(groups, MOM, 2, count, count)
    correlators, mine = pl.pallas_call(
        correlate_kernel,
        grid=(pairs.shape[0],),
        out_shape=(
            jax.ShapeDtypeStruct((pairs.shape[0], 2, MOM), jnp.float32),
            jax.ShapeDtypeStruct((share, count), jnp.float32),
        ),
        in_specs=[
            smem,
            vmem,
            pl.BlockSpec((1,) + perambulators.shape[1:], lambda n: (n, 0, 0, 0)),
            vmem,
        ],
        out_specs=(vmem, vmem),
        compiler_params=pltpu.CompilerParams(vmem_limit_bytes=VMEM_LIMIT),
        name="correlate",
    )(jnp.clip(pairs, 0, groups - 1), phi, perambulators, mine)
    return (mine, jnp.swapaxes(correlators, 1, 2))


def solution(mesh):
    return jax.shard_map(
        on_device,
        mesh=mesh,
        in_specs=(
            P(("groups", "slab"), None, None, None, None),
            P(("groups", "slab"), None, None, None, None, None),
            P(),
            P(),
            P(("groups", "slab"), None),
            P(("groups", "slab"), None, None, None),
        ),
        out_specs=(P(("groups", "slab"), None), P(("groups", "slab"), None, None)),
        check_vma=False,
    )
```
